32 devices in a mesh: row: 8 (over z, core), col: 4 (over y, x).
Axes of the slice: x: 2, y: 2, z: 4, core: 2. Of those that a mesh axis runs over, the one named last changes fastest.
Arguments:
- static_design: bfloat16 [128, 2048], P('col', 'row'), may hold values from -6 to 6
- tv_design: bfloat16 [128, 12288], P('row', 'col'), may hold values from -0.5 to 0.5
- taps: float32 [32], replicated, may hold values from -1 to 1
- arc_id: int32 [128], replicated, may hold values from 0 to 3, never falling along the last dimension, each value on 1 to 64 neighbouring positions
Outputs:
- normal_block: float32 [2048, 12288], P('row', 'col')
The draws below stay inside these ranges and needn't reach their ends.
Inputs may be any that keep to these rules, and one draw needn't show every extreme that they name: `arc_id`: arc numbers never fall along the rows; each arc has 1 to 64 rows and one has exactly 64.
All inputs are finite; a program needn't handle non-finite values.
Results may differ from the reference program's by a relative error of at most 0.0029.
Values may be sent and summed in bfloat16 or wider, within the bound.
A program may use at most 64 MiB of HBM per device.

```python
import math
import jax
import jax.numpy as jnp
import numpy as np
from jax import lax

TAPS = 32
ARCS = 4
S = 2048
TV = 12288
R = 128
ARC_MOST = 64


def level_of(rng, shape, cuts, low, largest):
    def one(axis_at, blocks):
        heights = jax.random.uniform(jax.random.fold_in(jax.random.fold_in(rng, 6), axis_at), (blocks,), jnp.float32, low / len(cuts), largest / len(cuts))
        return jnp.repeat(jnp.exp(heights), shape[axis_at] // blocks).reshape((-1,) + (1,) * (len(shape) - axis_at - 1))

    factor_of = one(*cuts[0])
    for cut in cuts[1:]:
        factor_of = factor_of * one(*cut)
    return factor_of


def profile(count, total, bound, skew):
    portions = [(1 << 20) // math.isqrt(rank ** skew) + 1 for rank in range(2, count + 1)]
    surplus, given = total - bound - (count - 1), [1] * (count - 1)
    while surplus > 0:
        movable = [i for i in range(count - 1) if given[i] < bound]
        mass, left = sum([portions[i] for i in movable]), surplus
        for i in movable:
            addition = min(bound - given[i], max(1, left * portions[i] // mass), surplus)
            given[i] = given[i] + addition
            surplus = surplus - addition
    return np.array([bound] + given)


def ragged(rng, number_of, total, bound, skew):
    if number_of == 2:
        one = jax.random.randint(rng, (), max(1, total - bound), min(bound, total - 1) + 1)
        return jnp.stack([one, total - one])
    sizes = jnp.asarray(profile(number_of, total, bound, skew), jnp.int32)
    pairs = (number_of - 1) // 2
    donor, receiver = sizes[1:1 + 2 * pairs:2], sizes[2:2 + 2 * pairs:2]
    slack = jnp.minimum(donor - 1, bound - receiver)
    passed = jax.random.randint(jax.random.fold_in(rng, 1), (pairs,), 0, 1 << 20) % (slack + 1)
    sizes = sizes.at[1:1 + 2 * pairs:2].set(donor - passed).at[2:2 + 2 * pairs:2].set(receiver + passed)
    return sizes[jax.random.permutation(jax.random.fold_in(rng, 2), number_of)]


def bell_draw(stream_key, shape, spread, bound, pieces=(), dtype=jnp.bfloat16):
    entries = spread * jax.random.normal(stream_key, shape, jnp.float32)
    if pieces:
        entries = entries * level_of(stream_key, shape, pieces, -0.22, 0.18)
    return jnp.clip(entries, -bound, bound).astype(dtype)


def setup_inputs(seed: int = 0) -> dict:
    key_list = jax.random.split(jax.random.key(seed), 5)
    return {
        "static_design": bell_draw(key_list[0], (R, S), 1.0, 6.0, ((0, 4), (1, 8))),
        "tv_design": bell_draw(key_list[1], (R, TV), R ** -0.5, 0.5, ((0, 8), (1, 4))),
        "taps": bell_draw(key_list[2], (TAPS,), 0.18, 1.0, (), jnp.float32),
        "arc_id": jnp.searchsorted(jnp.cumsum(ragged(key_list[3], ARCS, R, ARC_MOST, 0)), jnp.arange(R), side="right").astype(jnp.int32),
    }


def shift_down(values, steps, fill):
    pads = [(steps, 0)] + [(0, 0)] * (values.ndim - 1)
    return jnp.pad(values, pads, constant_values=fill)[: values.shape[0]]


def shift_up(values, steps, fill):
    pads = [(0, steps)] + [(0, 0)] * (values.ndim - 1)
    return jnp.pad(values, pads, constant_values=fill)[steps:]


def decorrelate(block, arcs, taps):
    count = taps.shape[0]
    forward = jnp.zeros(block.shape, jnp.float32)
    for step in range(count):
        same = (shift_down(arcs, step, -2) == arcs)[:, None]
        forward = forward + taps[step] * jnp.where(same, shift_down(block, step, 0.0), 0.0)
    backward = jnp.zeros(block.shape, jnp.float32)
    for step in range(count):
        same = (shift_up(arcs, step, -2) == arcs)[:, None]
        backward = backward + taps[step] * jnp.where(same, shift_up(forward, step, 0.0), 0.0)
    return backward


def reference(static_design, tv_design, taps, arc_id):
    edge = taps.shape[0] - 1
    block = jnp.pad(static_design.astype(jnp.float32), ((edge, edge), (0, 0)))
    arcs = jnp.pad(arc_id, (edge, edge), constant_values=-1)
    weighted = decorrelate(block, arcs, taps)[edge:-edge].astype(jnp.bfloat16)
    return lax.dot_general(weighted, tv_design, (((0,), (0,)), ((), ())), preferred_element_type=jnp.float32)
```

```python
import functools

import jax
import jax.numpy as jnp
from jax import lax
from jax.experimental import pallas as pl
from jax.experimental.pallas import tpu as pltpu
from jax.sharding import PartitionSpec as P

BLOCK = 128
MESH = pl.DeviceIdType.MESH
EXACT = lax.Precision.HIGHEST


def toeplitz(taps_ref, offset):
    shape = (BLOCK, BLOCK)
    lag = lax.broadcasted_iota(jnp.int32, shape, 0) - lax.broadcasted_iota(jnp.int32, shape, 1) + offset
    values = jnp.zeros(shape, jnp.float32)
    for step in range(taps_ref.shape[0]):
        values = jnp.where(lag == step, taps_ref[step], values)
    return values


def same_arc(rows, columns):
    shape = (BLOCK, BLOCK)
    down = jnp.transpose(jnp.broadcast_to(rows, shape))
    return down == jnp.broadcast_to(columns, shape)


def along(count, body, unrolled):
    if unrolled:
        for at in range(count):
            body(at)
    else:
        lax.fori_loop(0, count, lambda at, carry: (body(at), carry)[1], 0)


def kernel(
    n_row, n_col, pieces, taps_ref, arc_ref, static_ref, tv_ref, out_ref,
    static_all, tv_all, filter_ref, filtered_ref, weighted_ref,
    own_sem, static_send, static_recv, line_send, pair_send, tv_recv,
):
    row, col = lax.axis_index("row"), lax.axis_index("col")
    chips = n_row // 2
    chip, core = row // 2, row % 2
    static_rows, tv_rows = static_ref.shape[0], tv_ref.shape[0]
    width = tv_ref.shape[1] // pieces
    small = chips <= 4

    def at_row(chip_at, core_at):
        return (chip_at * 2 + core_at, col)

    has_up, has_down = chip < chips - 1, chip > 0

    barrier = pltpu.get_barrier_semaphore()
    for step in range(1, n_col):
        pl.semaphore_signal(barrier, inc=1, device_id=(row, (col + step) % n_col), device_id_type=MESH)
    pl.semaphore_signal(barrier, inc=1, device_id=at_row(chip, 1 - core), device_id_type=MESH)

    @pl.when(has_up)
    def _():
        pl.semaphore_signal(barrier, inc=1, device_id=at_row(chip + 1, core), device_id_type=MESH)

    @pl.when(has_down)
    def _():
        pl.semaphore_signal(barrier, inc=1, device_id=at_row(chip - 1, core), device_id_type=MESH)

    def static_rows_of(at):
        return static_all.at[pl.ds(pl.multiple_of(at * static_rows, static_rows), static_rows), :]

    def window(chip_at, core_at, piece):
        shard = chip_at * 2 + core_at
        rows = pl.ds(pl.multiple_of(shard * tv_rows, tv_rows), tv_rows)
        return tv_all.at[rows, pl.ds(piece * width, width)]

    def own_window(piece):
        return tv_ref.at[:, pl.ds(piece * width, width)]

    own_static = pltpu.make_async_copy(static_ref, static_rows_of(col), own_sem.at[0])
    own_tv = pltpu.make_async_copy(
        tv_ref, tv_all.at[pl.ds(pl.multiple_of(row * tv_rows, tv_rows), tv_rows), :], own_sem.at[1])
    own_static.start()
    own_tv.start()

    filter_ref[0] = toeplitz(taps_ref, 0)
    if arc_ref.shape[0] > 1:
        filter_ref[1] = toeplitz(taps_ref, BLOCK)

    pl.semaphore_wait(barrier, n_col + has_up.astype(jnp.int32) + has_down.astype(jnp.int32))

    def to_line(src, chip_at, piece, way):
        return pltpu.make_async_remote_copy(
            src_ref=src, dst_ref=window(chip_at, core, piece),
            send_sem=line_send.at[way, chip_at, piece], recv_sem=tv_recv.at[chip_at * 2 + core, piece],
            device_id=at_row(chip + 1 - 2 * way, core), device_id_type=MESH)

    def to_pair(src, chip_at, piece):
        return pltpu.make_async_remote_copy(
            src_ref=src, dst_ref=window(chip_at, core, piece),
            send_sem=pair_send.at[chip_at, piece], recv_sem=tv_recv.at[chip_at * 2 + core, piece],
            device_id=at_row(chip, 1 - core), device_id_type=MESH)

    def arrival(chip_at, core_at, piece):
        return pltpu.make_async_remote_copy(
            src_ref=window(chip_at, core_at, piece), dst_ref=window(chip_at, core_at, piece),
            send_sem=pair_send.at[chip_at, piece], recv_sem=tv_recv.at[chip_at * 2 + core_at, piece],
            device_id=at_row(chip, 1 - core), device_id_type=MESH)

    for piece in range(pieces):
        @pl.when(has_up)
        def _():
            to_line(own_window(piece), chip, piece, 0).start()

        @pl.when(has_down)
        def _():
            to_line(own_window(piece), chip, piece, 1).start()

    def to_col(step):
        peer = (col + step) % n_col
        return pltpu.make_async_remote_copy(
            src_ref=static_ref, dst_ref=static_rows_of(col),
            send_sem=static_send.at[step - 1], recv_sem=static_recv.at[step - 1],
            device_id=(row, peer), device_id_type=MESH)

    for step in range(1, n_col):
        to_col(step).start()
    for piece in range(pieces):
        to_pair(own_window(piece), chip, piece).start()

    def forward(hop, piece):
        below, above = chip - hop, chip + hop

        @pl.when(below >= 0)
        def _():
            arrival(below, core, piece).wait_recv()

            @pl.when(has_up)
            def _():
                to_line(window(below, core, piece), below, piece, 0).start()

            to_pair(window(below, core, piece), below, piece).start()

        @pl.when(above < chips)
        def _():
            arrival(above, core, piece).wait_recv()

            @pl.when(has_down)
            def _():
                to_line(window(above, core, piece), above, piece, 1).start()

            to_pair(window(above, core, piece), above, piece).start()

    def weigh():
        own_static.wait()
        for step in range(1, n_col):
            source = (col + n_col - step) % n_col
            pltpu.make_async_remote_copy(
                src_ref=static_ref, dst_ref=static_rows_of(source),
                send_sem=static_send.at[step - 1], recv_sem=static_recv.at[step - 1],
                device_id=(row, (col + step) % n_col), device_id_type=MESH).wait_recv()
        blocks = arc_ref.shape[0]
        contract = (((0,), (0,)), ((), ()))
        if blocks == 1:
            arcs = arc_ref[...]
            matrix = jnp.where(same_arc(arcs, arcs), filter_ref[0], 0.0)
            filtered = jnp.dot(matrix, static_all[...].astype(jnp.float32),
                               precision=EXACT, preferred_element_type=jnp.float32)
            weighted = lax.dot_general(filtered, matrix, contract,
                                       precision=EXACT, preferred_element_type=jnp.float32)
            weighted_ref[...] = weighted.astype(jnp.bfloat16)
            return

        def part(block, back):
            other = block - back
            inside = jnp.logical_and(other >= 0, block < blocks)
            here, there = jnp.minimum(block, blocks - 1), jnp.maximum(other, 0)
            arcs = same_arc(arc_ref[pl.ds(here, 1), :], arc_ref[pl.ds(there, 1), :])
            return jnp.where(jnp.logical_and(arcs, inside), filter_ref[back], 0.0)

        def rows_of(block):
            return pl.ds(pl.multiple_of(block * BLOCK, BLOCK), BLOCK)

        def first(block, carry):
            before = jnp.maximum(block - 1, 0)
            filtered_ref[rows_of(block), :] = jnp.dot(
                part(block, 0), static_all[rows_of(block), :].astype(jnp.float32),
                precision=EXACT, preferred_element_type=jnp.float32
            ) + jnp.dot(
                part(block, 1), static_all[rows_of(before), :].astype(jnp.float32),
                precision=EXACT, preferred_element_type=jnp.float32)
            return carry

        def second(block, carry):
            after = jnp.minimum(block + 1, blocks - 1)
            weighted = lax.dot_general(
                filtered_ref[rows_of(block), :], part(block, 0), contract,
                precision=EXACT, preferred_element_type=jnp.float32
            ) + lax.dot_general(
                filtered_ref[rows_of(after), :], part(block + 1, 1), contract,
                precision=EXACT, preferred_element_type=jnp.float32)
            weighted_ref[:, rows_of(block)] = weighted.astype(jnp.bfloat16)
            return carry

        lax.fori_loop(0, blocks, first, 0)
        lax.fori_loop(0, blocks, second, 0)

    def multiply(piece):
        def paired(chip_at):
            arrival(chip_at, 1 - core, piece).wait_recv()

        along(chips, paired, small)
        if piece == 0:
            own_tv.wait()
        columns = pl.ds(piece * width, width)
        out_ref[:, columns] = jnp.dot(
            weighted_ref[...], tv_all[:, columns], preferred_element_type=jnp.float32)

    for piece in range(pieces):
        forward(1, piece)
    weigh()

    def middle(at):
        for piece in range(pieces):
            forward(at + 2, piece)

    along(chips - 3, middle, small)
    for piece in range(pieces):
        forward(chips - 1, piece)
        if piece > 0:
            multiply(piece - 1)
    multiply(pieces - 1)

    for step in range(1, n_col):
        to_col(step).wait_send()

    def sent(chip_at):
        for piece in range(pieces):
            @pl.when(jnp.logical_and(has_up, chip_at <= chip))
            def _():
                to_line(own_window(piece), chip_at, piece, 0).wait_send()

            @pl.when(jnp.logical_and(has_down, chip_at >= chip))
            def _():
                to_line(own_window(piece), chip_at, piece, 1).wait_send()

            to_pair(own_window(piece), chip_at, piece).wait_send()

    along(chips, sent, small)


def body(static_design, tv_design, taps, arc_id, n_row, n_col):
    static_rows, static_width = static_design.shape
    tv_rows, tv_width = tv_design.shape
    rows = tv_rows * n_row
    pieces = 4 if n_row <= 8 else 1
    any_space = pl.BlockSpec(memory_space=pl.ANY)
    vmem = pl.BlockSpec(memory_space=pltpu.VMEM)
    return pl.pallas_call(
        functools.partial(kernel, n_row, n_col, pieces),
        out_shape=jax.ShapeDtypeStruct((static_width, tv_width), jnp.float32),
        in_specs=[pl.BlockSpec(memory_space=pltpu.SMEM), vmem, any_space, any_space],
        out_specs=vmem,
        scratch_shapes=[
            pltpu.VMEM((rows, static_width), jnp.bfloat16),
            pltpu.VMEM((rows, tv_width), jnp.bfloat16),
            pltpu.VMEM((2, BLOCK, BLOCK), jnp.float32),
            pltpu.VMEM((rows if rows > BLOCK else 8, static_width), jnp.float32),
            pltpu.VMEM((static_width, rows), jnp.bfloat16),
            pltpu.SemaphoreType.DMA((2,)),
            pltpu.SemaphoreType.DMA((n_col - 1,)),
            pltpu.SemaphoreType.DMA((n_col - 1,)),
            pltpu.SemaphoreType.DMA((2, n_row // 2, pieces)),
            pltpu.SemaphoreType.DMA((n_row // 2, pieces)),
            pltpu.SemaphoreType.DMA((n_row, pieces)),
        ],
        compiler_params=pltpu.CompilerParams(
            collective_id=0, has_side_effects=True, vmem_limit_bytes=40 * 1024 * 1024),
        cost_estimate=pl.CostEstimate(
            flops=2 * static_width * rows * tv_width, bytes_accessed=4 * static_width * tv_width, transcendentals=0),
    )(taps, arc_id.reshape(rows // BLOCK, BLOCK), static_design, tv_design)


def solution(mesh):
    return jax.shard_map(
        functools.partial(body, n_row=mesh.shape["row"], n_col=mesh.shape["col"]),
        mesh=mesh,
        in_specs=(P("col", "row"), P("row", "col"), P(), P()),
        out_specs=P("row", "col"),
        check_vma=False,
    )
```

```python
import functools

import jax
import jax.numpy as jnp
from jax import lax
from jax.experimental import pallas as pl
from jax.experimental.pallas import tpu as pltpu
from jax.sharding import PartitionSpec as P

BLOCK = 128
MESH = pl.DeviceIdType.MESH
EXACT = lax.Precision.HIGHEST


def toeplitz(taps_ref, offset, turned=False):
    shape = (BLOCK, BLOCK)
    lag = lax.broadcasted_iota(jnp.int32, shape, int(turned)) - lax.broadcasted_iota(jnp.int32, shape, 1 - turned) + offset
    values = jnp.zeros(shape, jnp.float32)
    for step in range(taps_ref.shape[0]):
        values = jnp.where(lag == step, taps_ref[step], values)
    return values


def same_arc(rows, columns):
    shape = (BLOCK, BLOCK)
    down = jnp.transpose(jnp.broadcast_to(rows, shape))
    return down == jnp.broadcast_to(columns, shape)


def along(count, body, unrolled):
    if unrolled:
        for at in range(count):
            body(at)
    else:
        lax.fori_loop(0, count, lambda at, carry: (body(at), carry)[1], 0)


def kernel(
    n_row, n_col, pieces, taps_hbm, arc_hbm, static_ref, tv_ref, out_ref,
    taps_ref, arc_ref, static_all, tv_all, filter_ref, filtered_ref, weighted_ref,
    own_sem, static_send, static_recv, line_send, pair_send, tv_recv,
):
    row, col = lax.axis_index("row"), lax.axis_index("col")
    chips = n_row // 2
    chip, core = row // 2, row % 2
    static_rows, tv_rows = static_ref.shape[0], tv_ref.shape[0]
    width = tv_ref.shape[1] // pieces
    small = chips <= 4

    def at_row(chip_at, core_at):
        return (chip_at * 2 + core_at, col)

    has_up, has_down = chip < chips - 1, chip > 0

    barrier = pltpu.get_barrier_semaphore()
    for step in range(1, n_col):
        pl.semaphore_signal(barrier, inc=1, device_id=(row, (col + step) % n_col), device_id_type=MESH)
    pl.semaphore_signal(barrier, inc=1, device_id=at_row(chip, 1 - core), device_id_type=MESH)

    @pl.when(has_up)
    def _():
        pl.semaphore_signal(barrier, inc=1, device_id=at_row(chip + 1, core), device_id_type=MESH)

    @pl.when(has_down)
    def _():
        pl.semaphore_signal(barrier, inc=1, device_id=at_row(chip - 1, core), device_id_type=MESH)

    def static_rows_of(at):
        return static_all.at[pl.ds(pl.multiple_of(at * static_rows, static_rows), static_rows), :]

    def window(chip_at, core_at, piece):
        shard = chip_at * 2 + core_at
        rows = pl.ds(pl.multiple_of(shard * tv_rows, tv_rows), tv_rows)
        return tv_all.at[rows, pl.ds(piece * width, width)]

    def own_window(piece):
        return tv_ref.at[:, pl.ds(piece * width, width)]

    own_static = pltpu.make_async_copy(static_ref, static_rows_of(col), own_sem.at[0])
    own_tv = pltpu.make_async_copy(
        tv_ref, tv_all.at[pl.ds(pl.multiple_of(row * tv_rows, tv_rows), tv_rows), :], own_sem.at[1])
    own_taps = pltpu.make_async_copy(taps_hbm, taps_ref, own_sem.at[2])
    own_arcs = pltpu.make_async_copy(arc_hbm, arc_ref, own_sem.at[3])
    own_taps.start()
    own_arcs.start()
    own_static.start()
    own_tv.start()

    own_taps.wait()
    own_arcs.wait()
    if arc_ref.shape[0] > 1:
        filter_ref[0] = toeplitz(taps_ref, 0)
        filter_ref[1] = toeplitz(taps_ref, BLOCK)
    else:
        same = same_arc(arc_ref[...], arc_ref[...])
        filter_ref[0] = jnp.where(same, toeplitz(taps_ref, 0), 0.0)
        filter_ref[1] = jnp.where(same, toeplitz(taps_ref, 0, True), 0.0)

    pl.semaphore_wait(barrier, n_col + has_up.astype(jnp.int32) + has_down.astype(jnp.int32))

    def to_line(src, chip_at, piece, way):
        return pltpu.make_async_remote_copy(
            src_ref=src, dst_ref=window(chip_at, core, piece),
            send_sem=line_send.at[way, chip_at, piece], recv_sem=tv_recv.at[chip_at * 2 + core, piece],
            device_id=at_row(chip + 1 - 2 * way, core), device_id_type=MESH)

    def to_pair(src, chip_at, piece):
        return pltpu.make_async_remote_copy(
            src_ref=src, dst_ref=window(chip_at, core, piece),
            send_sem=pair_send.at[chip_at, piece], recv_sem=tv_recv.at[chip_at * 2 + core, piece],
            device_id=at_row(chip, 1 - core), device_id_type=MESH)

    def arrival(chip_at, core_at, piece):
        return pltpu.make_async_remote_copy(
            src_ref=window(chip_at, core_at, piece), dst_ref=window(chip_at, core_at, piece),
            send_sem=pair_send.at[chip_at, piece], recv_sem=tv_recv.at[chip_at * 2 + core_at, piece],
            device_id=at_row(chip, 1 - core), device_id_type=MESH)

    def to_col(step):
        peer = (col + step) % n_col
        return pltpu.make_async_remote_copy(
            src_ref=static_ref, dst_ref=static_rows_of(col),
            send_sem=static_send.at[step - 1], recv_sem=static_recv.at[step - 1],
            device_id=(row, peer), device_id_type=MESH)

    for step in range(1, n_col):
        to_col(step).start()
    for piece in range(pieces):
        @pl.when(has_up)
        def _():
            to_line(own_window(piece), chip, piece, 0).start()

        @pl.when(has_down)
        def _():
            to_line(own_window(piece), chip, piece, 1).start()

    for piece in range(pieces):
        to_pair(own_window(piece), chip, piece).start()

    def forward(hop, piece):
        below, above = chip - hop, chip + hop

        @pl.when(below >= 0)
        def _():
            arrival(below, core, piece).wait_recv()

            @pl.when(has_up)
            def _():
                to_line(window(below, core, piece), below, piece, 0).start()

            to_pair(window(below, core, piece), below, piece).start()

        @pl.when(above < chips)
        def _():
            arrival(above, core, piece).wait_recv()

            @pl.when(has_down)
            def _():
                to_line(window(above, core, piece), above, piece, 1).start()

            to_pair(window(above, core, piece), above, piece).start()

    def weigh():
        own_static.wait()
        for step in range(1, n_col):
            source = (col + n_col - step) % n_col
            pltpu.make_async_remote_copy(
                src_ref=static_ref, dst_ref=static_rows_of(source),
                send_sem=static_send.at[step - 1], recv_sem=static_recv.at[step - 1],
                device_id=(row, (col + step) % n_col), device_id_type=MESH).wait_recv()
        blocks = arc_ref.shape[0]
        contract = (((0,), (0,)), ((), ()))
        if blocks == 1:
            filtered = lax.dot_general(static_all[...].astype(jnp.float32), filter_ref[1], contract,
                                       precision=EXACT, preferred_element_type=jnp.float32)
            weighted = jnp.dot(filtered, filter_ref[0], precision=EXACT, preferred_element_type=jnp.float32)
            weighted_ref[...] = weighted.astype(jnp.bfloat16)
            return

        def part(block, back):
            other = block - back
            inside = jnp.logical_and(other >= 0, block < blocks)
            here, there = jnp.minimum(block, blocks - 1), jnp.maximum(other, 0)
            arcs = same_arc(arc_ref[pl.ds(here, 1), :], arc_ref[pl.ds(there, 1), :])
            return jnp.where(jnp.logical_and(arcs, inside), filter_ref[back], 0.0)

        def rows_of(block):
            return pl.ds(pl.multiple_of(block * BLOCK, BLOCK), BLOCK)

        def first(block, carry):
            before = jnp.maximum(block - 1, 0)
            filtered_ref[rows_of(block), :] = jnp.dot(
                part(block, 0), static_all[rows_of(block), :].astype(jnp.float32),
                precision=EXACT, preferred_element_type=jnp.float32
            ) + jnp.dot(
                part(block, 1), static_all[rows_of(before), :].astype(jnp.float32),
                precision=EXACT, preferred_element_type=jnp.float32)
            return carry

        def second(block, carry):
            after = jnp.minimum(block + 1, blocks - 1)
            weighted = lax.dot_general(
                filtered_ref[rows_of(block), :], part(block, 0), contract,
                precision=EXACT, preferred_element_type=jnp.float32
            ) + lax.dot_general(
                filtered_ref[rows_of(after), :], part(block + 1, 1), contract,
                precision=EXACT, preferred_element_type=jnp.float32)
            weighted_ref[:, rows_of(block)] = weighted.astype(jnp.bfloat16)
            return carry

        lax.fori_loop(0, blocks, first, 0)
        lax.fori_loop(0, blocks, second, 0)

    def multiply(piece):
        def paired(chip_at):
            arrival(chip_at, 1 - core, piece).wait_recv()

        along(chips, paired, small)
        if piece == 0:
            own_tv.wait()
        columns = pl.ds(piece * width, width)
        out_ref[:, columns] = jnp.dot(
            weighted_ref[...], tv_all[:, columns], preferred_element_type=jnp.float32)

    for piece in range(pieces):
        forward(1, piece)

    def middle(at):
        for piece in range(pieces):
            forward(at + 2, piece)

    along(chips - 3, middle, small)
    weigh()
    for piece in range(pieces):
        forward(chips - 1, piece)
        if piece > 0:
            multiply(piece - 1)
    multiply(pieces - 1)

    for step in range(1, n_col):
        to_col(step).wait_send()

    def sent(chip_at):
        for piece in range(pieces):
            @pl.when(jnp.logical_and(has_up, chip_at <= chip))
            def _():
                to_line(own_window(piece), chip_at, piece, 0).wait_send()

            @pl.when(jnp.logical_and(has_down, chip_at >= chip))
            def _():
                to_line(own_window(piece), chip_at, piece, 1).wait_send()

            to_pair(own_window(piece), chip_at, piece).wait_send()

    along(chips, sent, small)


def body(static_design, tv_design, taps, arc_id, n_row, n_col):
    static_rows, static_width = static_design.shape
    tv_rows, tv_width = tv_design.shape
    rows = tv_rows * n_row
    pieces = 4 if n_row <= 8 else 1
    hbm = pl.BlockSpec(memory_space=pltpu.HBM)
    operands = (taps, arc_id.reshape(rows // BLOCK, BLOCK), static_design, tv_design)
    vmem = pl.BlockSpec(memory_space=pltpu.VMEM)
    return pl.pallas_call(
        functools.partial(kernel, n_row, n_col, pieces),
        out_shape=jax.ShapeDtypeStruct((static_width, tv_width), jnp.float32),
        in_specs=[hbm, hbm, hbm, hbm],
        out_specs=vmem,
        scratch_shapes=[
            pltpu.SMEM(taps.shape, jnp.float32),
            pltpu.VMEM((rows // BLOCK, BLOCK), jnp.int32),
            pltpu.VMEM((rows, static_width), jnp.bfloat16),
            pltpu.VMEM((rows, tv_width), jnp.bfloat16),
            pltpu.VMEM((2, BLOCK, BLOCK), jnp.float32),
            pltpu.VMEM((rows if rows > BLOCK else 8, static_width), jnp.float32),
            pltpu.VMEM((static_width, rows), jnp.bfloat16),
            pltpu.SemaphoreType.DMA((4,)),
            pltpu.SemaphoreType.DMA((n_col - 1,)),
            pltpu.SemaphoreType.DMA((n_col - 1,)),
            pltpu.SemaphoreType.DMA((2, n_row // 2, pieces)),
            pltpu.SemaphoreType.DMA((n_row // 2, pieces)),
            pltpu.SemaphoreType.DMA((n_row, pieces)),
        ],
        compiler_params=pltpu.CompilerParams(
            collective_id=0, has_side_effects=True, vmem_limit_bytes=40 * 1024 * 1024),
        cost_estimate=pl.CostEstimate(
            flops=2 * static_width * rows * tv_width, bytes_accessed=4 * static_width * tv_width, transcendentals=0),
    )(*(pltpu.with_memory_space_constraint(value, pltpu.HBM) for value in operands))


def solution(mesh):
    return jax.shard_map(
        functools.partial(body, n_row=mesh.shape["row"], n_col=mesh.shape["col"]),
        mesh=mesh,
        in_specs=(P("col", "row"), P("row", "col"), P(), P()),
        out_specs=P("row", "col"),
        check_vma=False,
    )
```

```python
import functools

import jax
import jax.numpy as jnp
from jax import lax
from jax.experimental import pallas as pl
from jax.experimental.pallas import tpu as pltpu
from jax.sharding import PartitionSpec as P

BLOCK = 128
MESH = pl.DeviceIdType.MESH
EXACT = lax.Precision.HIGHEST


def toeplitz(taps_ref, offset, turned=False):
    shape = (BLOCK, BLOCK)
    lag = lax.broadcasted_iota(jnp.int32, shape, int(turned)) - lax.broadcasted_iota(jnp.int32, shape, 1 - turned) + offset
    values = jnp.zeros(shape, jnp.float32)
    for step in range(taps_ref.shape[0]):
        values = jnp.where(lag == step, taps_ref[step], values)
    return values


def same_arc(rows, columns):
    shape = (BLOCK, BLOCK)
    down = jnp.transpose(jnp.broadcast_to(rows, shape))
    return down == jnp.broadcast_to(columns, shape)


def along(count, body, unrolled):
    if unrolled:
        for at in range(count):
            body(at)
    else:
        lax.fori_loop(0, count, lambda at, carry: (body(at), carry)[1], 0)


def kernel(
    n_row, n_col, pieces, taps_hbm, arc_hbm, static_ref, tv_ref, out_ref,
    taps_ref, arc_ref, static_all, tv_all, filter_ref, filtered_ref, weighted_ref,
    own_sem, static_send, static_recv, line_send, pair_send, tv_recv,
):
    row, col = lax.axis_index("row"), lax.axis_index("col")
    chips = n_row // 2
    chip, core = row // 2, row % 2
    static_rows, tv_rows = static_ref.shape[0], tv_ref.shape[0]
    width = tv_ref.shape[1] // pieces
    small = chips <= 4

    def at_row(chip_at, core_at):
        return (chip_at * 2 + core_at, col)


    barrier = pltpu.get_barrier_semaphore()
    for step in range(1, n_col):
        pl.semaphore_signal(barrier, inc=1, device_id=(row, (col + step) % n_col), device_id_type=MESH)
    pl.semaphore_signal(barrier, inc=1, device_id=at_row(chip, 1 - core), device_id_type=MESH)

    along(chips - 1, lambda at: pl.semaphore_signal(
        barrier, inc=1, device_id=at_row((chip + at + 1) % chips, core), device_id_type=MESH), small)

    def static_rows_of(at):
        return static_all.at[pl.ds(pl.multiple_of(at * static_rows, static_rows), static_rows), :]

    def window(chip_at, core_at, piece):
        shard = chip_at * 2 + core_at
        rows = pl.ds(pl.multiple_of(shard * tv_rows, tv_rows), tv_rows)
        return tv_all.at[rows, pl.ds(piece * width, width)]

    def own_window(piece):
        return tv_ref.at[:, pl.ds(piece * width, width)]

    own_static = pltpu.make_async_copy(static_ref, static_rows_of(col), own_sem.at[0])
    own_tv = pltpu.make_async_copy(
        tv_ref, tv_all.at[pl.ds(pl.multiple_of(row * tv_rows, tv_rows), tv_rows), :], own_sem.at[1])
    own_taps = pltpu.make_async_copy(taps_hbm, taps_ref, own_sem.at[2])
    own_arcs = pltpu.make_async_copy(arc_hbm, arc_ref, own_sem.at[3])
    own_taps.start()
    own_arcs.start()
    own_static.start()
    own_tv.start()

    pl.semaphore_wait(barrier, n_col + chips - 1)

    def to_line(src, chip_at, piece, way):
        return pltpu.make_async_remote_copy(
            src_ref=src, dst_ref=window(chip_at, core, piece),
            send_sem=line_send.at[way, chip_at, piece], recv_sem=tv_recv.at[chip_at * 2 + core, piece],
            device_id=at_row(chip + 1 - 2 * way, core), device_id_type=MESH)

    def to_pair(src, chip_at, piece):
        return pltpu.make_async_remote_copy(
            src_ref=src, dst_ref=window(chip_at, core, piece),
            send_sem=pair_send.at[chip_at, piece], recv_sem=tv_recv.at[chip_at * 2 + core, piece],
            device_id=at_row(chip, 1 - core), device_id_type=MESH)

    def arrival(chip_at, core_at, piece):
        return pltpu.make_async_remote_copy(
            src_ref=window(chip_at, core_at, piece), dst_ref=window(chip_at, core_at, piece),
            send_sem=pair_send.at[chip_at, piece], recv_sem=tv_recv.at[chip_at * 2 + core_at, piece],
            device_id=at_row(chip, 1 - core), device_id_type=MESH)

    def to_col(step):
        peer = (col + step) % n_col
        return pltpu.make_async_remote_copy(
            src_ref=static_ref, dst_ref=static_rows_of(col),
            send_sem=static_send.at[step - 1], recv_sem=static_recv.at[step - 1],
            device_id=(row, peer), device_id_type=MESH)

    for step in range(1, n_col):
        to_col(step).start()
    def to_chip(target, piece):
        return pltpu.make_async_remote_copy(
            src_ref=own_window(piece), dst_ref=window(chip, core, piece),
            send_sem=line_send.at[2, target, piece], recv_sem=tv_recv.at[chip * 2 + core, piece],
            device_id=at_row(target, core), device_id_type=MESH)

    def pushes(target):
        inside = jnp.logical_and(target >= 0, jnp.logical_and(target < chips, target != chip))
        low = jnp.logical_and(target == 0, chip == 2)
        high = jnp.logical_and(target == chips - 1, chip == chips - 3)
        return jnp.logical_and(inside, jnp.logical_not(jnp.logical_or(low, high)))

    def push(at):
        distance = at + 1
        for target in (chip - distance, chip + distance):
            @pl.when(pushes(target))
            def _():
                for piece in range(pieces):
                    to_chip(target, piece).start()

    along(chips - 1, push, small)
    for piece in range(pieces):
        to_pair(own_window(piece), chip, piece).start()

    own_taps.wait()
    own_arcs.wait()
    if arc_ref.shape[0] > 1:
        filter_ref[0] = toeplitz(taps_ref, 0)
        filter_ref[1] = toeplitz(taps_ref, BLOCK)
    else:
        same = same_arc(arc_ref[...], arc_ref[...])
        filter_ref[0] = jnp.where(same, toeplitz(taps_ref, 0), 0.0)
        filter_ref[1] = jnp.where(same, toeplitz(taps_ref, 0, True), 0.0)

    def forward(hop, piece):
        below, above = chip - hop, chip + hop

        @pl.when(below >= 0)
        def _():
            arrival(below, core, piece).wait_recv()

            @pl.when(jnp.logical_and(chip == chips - 2, hop == 1))
            def _():
                to_line(window(below, core, piece), below, piece, 0).start()

            to_pair(window(below, core, piece), below, piece).start()

        @pl.when(above < chips)
        def _():
            arrival(above, core, piece).wait_recv()

            @pl.when(jnp.logical_and(chip == 1, hop == 1))
            def _():
                to_line(window(above, core, piece), above, piece, 1).start()

            to_pair(window(above, core, piece), above, piece).start()

    def weigh():
        own_static.wait()
        for step in range(1, n_col):
            source = (col + n_col - step) % n_col
            pltpu.make_async_remote_copy(
                src_ref=static_ref, dst_ref=static_rows_of(source),
                send_sem=static_send.at[step - 1], recv_sem=static_recv.at[step - 1],
                device_id=(row, (col + step) % n_col), device_id_type=MESH).wait_recv()
        blocks = arc_ref.shape[0]
        contract = (((0,), (0,)), ((), ()))
        if blocks == 1:
            filtered = lax.dot_general(static_all[...].astype(jnp.float32), filter_ref[1], contract,
                                       precision=EXACT, preferred_element_type=jnp.float32)
            weighted = jnp.dot(filtered, filter_ref[0], precision=EXACT, preferred_element_type=jnp.float32)
            weighted_ref[...] = weighted.astype(jnp.bfloat16)
            return

        def part(block, back):
            other = block - back
            inside = jnp.logical_and(other >= 0, block < blocks)
            here, there = jnp.minimum(block, blocks - 1), jnp.maximum(other, 0)
            arcs = same_arc(arc_ref[pl.ds(here, 1), :], arc_ref[pl.ds(there, 1), :])
            return jnp.where(jnp.logical_and(arcs, inside), filter_ref[back], 0.0)

        def rows_of(block):
            return pl.ds(pl.multiple_of(block * BLOCK, BLOCK), BLOCK)

        def first(block, carry):
            before = jnp.maximum(block - 1, 0)
            filtered_ref[rows_of(block), :] = jnp.dot(
                part(block, 0), static_all[rows_of(block), :].astype(jnp.float32),
                precision=EXACT, preferred_element_type=jnp.float32
            ) + jnp.dot(
                part(block, 1), static_all[rows_of(before), :].astype(jnp.float32),
                precision=EXACT, preferred_element_type=jnp.float32)
            return carry

        def second(block, carry):
            after = jnp.minimum(block + 1, blocks - 1)
            weighted = lax.dot_general(
                filtered_ref[rows_of(block), :], part(block, 0), contract,
                precision=EXACT, preferred_element_type=jnp.float32
            ) + lax.dot_general(
                filtered_ref[rows_of(after), :], part(block + 1, 1), contract,
                precision=EXACT, preferred_element_type=jnp.float32)
            weighted_ref[:, rows_of(block)] = weighted.astype(jnp.bfloat16)
            return carry

        lax.fori_loop(0, blocks, first, 0)
        lax.fori_loop(0, blocks, second, 0)

    def multiply(piece):
        def paired(chip_at):
            arrival(chip_at, 1 - core, piece).wait_recv()

        along(chips, paired, small)
        if piece == 0:
            own_tv.wait()
        columns = pl.ds(piece * width, width)
        out_ref[:, columns] = jnp.dot(
            weighted_ref[...], tv_all[:, columns], preferred_element_type=jnp.float32)

    for piece in range(pieces):
        forward(1, piece)

    def middle(at):
        for piece in range(pieces):
            forward(at + 2, piece)

    along(chips - 3, middle, small)
    weigh()
    for piece in range(pieces):
        forward(chips - 1, piece)
        if piece > 0:
            multiply(piece - 1)
    multiply(pieces - 1)

    for step in range(1, n_col):
        to_col(step).wait_send()

    def sent(chip_at):
        for piece in range(pieces):
            @pl.when(pushes(chip_at))
            def _():
                to_chip(chip_at, piece).wait_send()

            to_pair(own_window(piece), chip_at, piece).wait_send()

    along(chips, sent, small)
    for piece in range(pieces):
        @pl.when(chip == 1)
        def _():
            to_line(own_window(piece), 2, piece, 1).wait_send()

        @pl.when(chip == chips - 2)
        def _():
            to_line(own_window(piece), chips - 3, piece, 0).wait_send()


def body(static_design, tv_design, taps, arc_id, n_row, n_col):
    static_rows, static_width = static_design.shape
    tv_rows, tv_width = tv_design.shape
    rows = tv_rows * n_row
    pieces = 2 if n_row <= 8 else 1
    hbm = pl.BlockSpec(memory_space=pltpu.HBM)
    operands = (taps, arc_id.reshape(rows // BLOCK, BLOCK), static_design, tv_design)
    vmem = pl.BlockSpec(memory_space=pltpu.VMEM)
    return pl.pallas_call(
        functools.partial(kernel, n_row, n_col, pieces),
        out_shape=jax.ShapeDtypeStruct((static_width, tv_width), jnp.float32),
        in_specs=[hbm, hbm, hbm, hbm],
        out_specs=vmem,
        scratch_shapes=[
            pltpu.SMEM(taps.shape, jnp.float32),
            pltpu.VMEM((rows // BLOCK, BLOCK), jnp.int32),
            pltpu.VMEM((rows, static_width), jnp.bfloat16),
            pltpu.VMEM((rows, tv_width), jnp.bfloat16),
            pltpu.VMEM((2, BLOCK, BLOCK), jnp.float32),
            pltpu.VMEM((rows if rows > BLOCK else 8, static_width), jnp.float32),
            pltpu.VMEM((static_width, rows), jnp.bfloat16),
            pltpu.SemaphoreType.DMA((4,)),
            pltpu.SemaphoreType.DMA((n_col - 1,)),
            pltpu.SemaphoreType.DMA((n_col - 1,)),
            pltpu.SemaphoreType.DMA((3, n_row // 2, pieces)),
            pltpu.SemaphoreType.DMA((n_row // 2, pieces)),
            pltpu.SemaphoreType.DMA((n_row, pieces)),
        ],
        compiler_params=pltpu.CompilerParams(
            collective_id=0, has_side_effects=True, vmem_limit_bytes=40 * 1024 * 1024),
        cost_estimate=pl.CostEstimate(
            flops=2 * static_width * rows * tv_width, bytes_accessed=4 * static_width * tv_width, transcendentals=0),
    )(*(pltpu.with_memory_space_constraint(value, pltpu.HBM) for value in operands))


def solution(mesh):
    return jax.shard_map(
        functools.partial(body, n_row=mesh.shape["row"], n_col=mesh.shape["col"]),
        mesh=mesh,
        in_specs=(P("col", "row"), P("row", "col"), P(), P()),
        out_specs=P("row", "col"),
        check_vma=False,
    )
```

```python
import functools

import jax
import jax.numpy as jnp
from jax import lax
from jax.experimental import pallas as pl
from jax.experimental.pallas import tpu as pltpu
from jax.sharding import PartitionSpec as P

BLOCK = 128
MESH = pl.DeviceIdType.MESH
EXACT = lax.Precision.HIGHEST


def toeplitz(taps_ref, offset, turned=False):
    shape = (BLOCK, BLOCK)
    lag = lax.broadcasted_iota(jnp.int32, shape, int(turned)) - lax.broadcasted_iota(jnp.int32, shape, 1 - turned) + offset
    values = jnp.zeros(shape, jnp.float32)
    for step in range(taps_ref.shape[0]):
        values = jnp.where(lag == step, taps_ref[step], values)
    return values


def same_arc(rows, columns):
    shape = (BLOCK, BLOCK)
    down = jnp.transpose(jnp.broadcast_to(rows, shape))
    return down == jnp.broadcast_to(columns, shape)


def along(count, body, unrolled):
    if unrolled:
        for at in range(count):
            body(at)
    else:
        lax.fori_loop(0, count, lambda at, carry: (body(at), carry)[1], 0)


def kernel(
    n_row, n_col, pieces, taps_hbm, arc_hbm, static_ref, tv_ref, weighted_ref, tv_all,
    taps_ref, arc_ref, static_all, filter_ref, filtered_ref,
    own_sem, static_send, static_recv, line_send, pair_send, tv_recv,
):
    row, col = lax.axis_index("row"), lax.axis_index("col")
    chips = n_row // 2
    chip, core = row // 2, row % 2
    static_rows, tv_rows = static_ref.shape[0], tv_ref.shape[0]
    width = tv_ref.shape[1] // pieces
    small = chips <= 4

    def at_row(chip_at, core_at):
        return (chip_at * 2 + core_at, col)


    barrier = pltpu.get_barrier_semaphore()
    for step in range(1, n_col):
        pl.semaphore_signal(barrier, inc=1, device_id=(row, (col + step) % n_col), device_id_type=MESH)
    pl.semaphore_signal(barrier, inc=1, device_id=at_row(chip, 1 - core), device_id_type=MESH)

    along(chips - 1, lambda at: pl.semaphore_signal(
        barrier, inc=1, device_id=at_row((chip + at + 1) % chips, core), device_id_type=MESH), small)

    def static_rows_of(at):
        return static_all.at[pl.ds(pl.multiple_of(at * static_rows, static_rows), static_rows), :]

    def window(chip_at, core_at, piece):
        shard = chip_at * 2 + core_at
        rows = pl.ds(pl.multiple_of(shard * tv_rows, tv_rows), tv_rows)
        return tv_all.at[rows, pl.ds(piece * width, width)]

    def own_window(piece):
        return tv_ref.at[:, pl.ds(piece * width, width)]

    own_static = pltpu.make_async_copy(static_ref, static_rows_of(col), own_sem.at[0])
    own_tv = pltpu.make_async_copy(
        tv_ref, tv_all.at[pl.ds(pl.multiple_of(row * tv_rows, tv_rows), tv_rows), :], own_sem.at[1])
    own_taps = pltpu.make_async_copy(taps_hbm, taps_ref, own_sem.at[2])
    own_arcs = pltpu.make_async_copy(arc_hbm, arc_ref, own_sem.at[3])
    own_taps.start()
    own_arcs.start()
    own_static.start()
    own_tv.start()

    pl.semaphore_wait(barrier, n_col + chips - 1)

    def to_line(src, chip_at, piece, way):
        return pltpu.make_async_remote_copy(
            src_ref=src, dst_ref=window(chip_at, core, piece),
            send_sem=line_send.at[way, chip_at, piece], recv_sem=tv_recv.at[chip_at * 2 + core, piece],
            device_id=at_row(chip + 1 - 2 * way, core), device_id_type=MESH)

    def to_pair(src, chip_at, piece):
        return pltpu.make_async_remote_copy(
            src_ref=src, dst_ref=window(chip_at, core, piece),
            send_sem=pair_send.at[chip_at, piece], recv_sem=tv_recv.at[chip_at * 2 + core, piece],
            device_id=at_row(chip, 1 - core), device_id_type=MESH)

    def arrival(chip_at, core_at, piece):
        return pltpu.make_async_remote_copy(
            src_ref=window(chip_at, core_at, piece), dst_ref=window(chip_at, core_at, piece),
            send_sem=pair_send.at[chip_at, piece], recv_sem=tv_recv.at[chip_at * 2 + core_at, piece],
            device_id=at_row(chip, 1 - core), device_id_type=MESH)

    def to_col(step):
        peer = (col + step) % n_col
        return pltpu.make_async_remote_copy(
            src_ref=static_ref, dst_ref=static_rows_of(col),
            send_sem=static_send.at[step - 1], recv_sem=static_recv.at[step - 1],
            device_id=(row, peer), device_id_type=MESH)

    def to_chip(target, piece):
        return pltpu.make_async_remote_copy(
            src_ref=own_window(piece), dst_ref=window(chip, core, piece),
            send_sem=line_send.at[2, target, piece], recv_sem=tv_recv.at[chip * 2 + core, piece],
            device_id=at_row(target, core), device_id_type=MESH)

    def pushes(target):
        inside = jnp.logical_and(target >= 0, jnp.logical_and(target < chips, target != chip))
        low = jnp.logical_and(target == 0, chip == 2)
        high = jnp.logical_and(target == chips - 1, chip == chips - 3)
        return jnp.logical_and(inside, jnp.logical_not(jnp.logical_or(low, high)))

    def push(at):
        distance = at + 1
        for target in (chip - distance, chip + distance):
            @pl.when(pushes(target))
            def _():
                for piece in range(pieces):
                    to_chip(target, piece).start()

    push(0)

    for piece in range(pieces):
        to_pair(own_window(piece), chip, piece).start()

    for step in range(1, n_col):
        to_col(step).start()

    along(chips - 2, lambda at: push(at + 1), small)

    def forward(hop, piece):
        below, above = chip - hop, chip + hop

        @pl.when(below >= 0)
        def _():
            arrival(below, core, piece).wait_recv()

            @pl.when(jnp.logical_and(chip == chips - 2, hop == 1))
            def _():
                to_line(window(below, core, piece), below, piece, 0).start()

            to_pair(window(below, core, piece), below, piece).start()

        @pl.when(above < chips)
        def _():
            arrival(above, core, piece).wait_recv()

            @pl.when(jnp.logical_and(chip == 1, hop == 1))
            def _():
                to_line(window(above, core, piece), above, piece, 1).start()

            to_pair(window(above, core, piece), above, piece).start()

    def weigh():
        own_static.wait()
        for step in range(1, n_col):
            source = (col + n_col - step) % n_col
            pltpu.make_async_remote_copy(
                src_ref=static_ref, dst_ref=static_rows_of(source),
                send_sem=static_send.at[step - 1], recv_sem=static_recv.at[step - 1],
                device_id=(row, (col + step) % n_col), device_id_type=MESH).wait_recv()
        blocks = arc_ref.shape[0]
        contract = (((0,), (0,)), ((), ()))
        if blocks == 1:
            filtered = lax.dot_general(static_all[...].astype(jnp.float32), filter_ref[1], contract,
                                       precision=EXACT, preferred_element_type=jnp.float32)
            weighted = jnp.dot(filtered, filter_ref[0], precision=EXACT, preferred_element_type=jnp.float32)
            weighted_ref[...] = weighted.astype(jnp.bfloat16)
            return

        def part(block, back):
            other = block - back
            inside = jnp.logical_and(other >= 0, block < blocks)
            here, there = jnp.minimum(block, blocks - 1), jnp.maximum(other, 0)
            arcs = same_arc(arc_ref[pl.ds(here, 1), :], arc_ref[pl.ds(there, 1), :])
            return jnp.where(jnp.logical_and(arcs, inside), filter_ref[back], 0.0)

        def rows_of(block):
            return pl.ds(pl.multiple_of(block * BLOCK, BLOCK), BLOCK)

        def first(block, carry):
            before = jnp.maximum(block - 1, 0)
            filtered_ref[rows_of(block), :] = jnp.dot(
                part(block, 0), static_all[rows_of(block), :].astype(jnp.float32),
                precision=EXACT, preferred_element_type=jnp.float32
            ) + jnp.dot(
                part(block, 1), static_all[rows_of(before), :].astype(jnp.float32),
                precision=EXACT, preferred_element_type=jnp.float32)
            return carry

        def second(block, carry):
            after = jnp.minimum(block + 1, blocks - 1)
            weighted = lax.dot_general(
                filtered_ref[rows_of(block), :], part(block, 0), contract,
                precision=EXACT, preferred_element_type=jnp.float32
            ) + lax.dot_general(
                filtered_ref[rows_of(after), :], part(block + 1, 1), contract,
                precision=EXACT, preferred_element_type=jnp.float32)
            weighted_ref[:, rows_of(block)] = weighted.astype(jnp.bfloat16)
            return carry

        lax.fori_loop(0, blocks, first, 0)
        lax.fori_loop(0, blocks, second, 0)

    def multiply(piece):
        def paired(chip_at):
            arrival(chip_at, 1 - core, piece).wait_recv()

        along(chips, paired, small)
        if piece == 0:
            own_tv.wait()

    for piece in range(pieces):
        forward(1, piece)

    own_taps.wait()
    own_arcs.wait()
    if arc_ref.shape[0] > 1:
        filter_ref[0] = toeplitz(taps_ref, 0)
        filter_ref[1] = toeplitz(taps_ref, BLOCK)
    else:
        same = same_arc(arc_ref[...], arc_ref[...])
        filter_ref[0] = jnp.where(same, toeplitz(taps_ref, 0), 0.0)
        filter_ref[1] = jnp.where(same, toeplitz(taps_ref, 0, True), 0.0)

    def middle(at):
        for piece in range(pieces):
            forward(at + 2, piece)

    along(chips - 3, middle, small)
    weigh()
    for piece in range(pieces):
        forward(chips - 1, piece)
        if piece > 0:
            multiply(piece - 1)
    multiply(pieces - 1)

    for step in range(1, n_col):
        to_col(step).wait_send()

    def sent(chip_at):
        for piece in range(pieces):
            @pl.when(pushes(chip_at))
            def _():
                to_chip(chip_at, piece).wait_send()

            to_pair(own_window(piece), chip_at, piece).wait_send()

    along(chips, sent, small)
    for piece in range(pieces):
        @pl.when(chip == 1)
        def _():
            to_line(own_window(piece), 2, piece, 1).wait_send()

        @pl.when(chip == chips - 2)
        def _():
            to_line(own_window(piece), chips - 3, piece, 0).wait_send()


def multiply_out(pieces, weighted_ref, tv_ref, out_ref, held, sems):
    width = tv_ref.shape[1] // pieces
    copies = []
    for piece in range(pieces):
        columns = pl.ds(piece * width, width)
        held[:, columns] = jnp.dot(weighted_ref[...], tv_ref[:, columns], preferred_element_type=jnp.float32)
        copies.append(pltpu.make_async_copy(held.at[:, columns], out_ref.at[:, columns], sems.at[piece]))
        copies[-1].start()
    for copy in copies:
        copy.wait()


def body(static_design, tv_design, taps, arc_id, n_row, n_col):
    static_rows, static_width = static_design.shape
    tv_rows, tv_width = tv_design.shape
    rows = tv_rows * n_row
    pieces = 2 if n_row <= 8 else 1
    hbm = pl.BlockSpec(memory_space=pltpu.HBM)
    operands = (taps, arc_id.reshape(rows // BLOCK, BLOCK), static_design, tv_design)
    vmem = pl.BlockSpec(memory_space=pltpu.VMEM)
    weighted, gathered = pl.pallas_call(
        functools.partial(kernel, n_row, n_col, pieces),
        out_shape=(jax.ShapeDtypeStruct((static_width, rows), jnp.bfloat16), jax.ShapeDtypeStruct((rows, tv_width), jnp.bfloat16)),
        in_specs=[hbm, hbm, hbm, hbm],
        out_specs=(vmem, vmem),
        scratch_shapes=[
            pltpu.SMEM(taps.shape, jnp.float32),
            pltpu.VMEM((rows // BLOCK, BLOCK), jnp.int32),
            pltpu.VMEM((rows, static_width), jnp.bfloat16),
            pltpu.VMEM((2, BLOCK, BLOCK), jnp.float32),
            pltpu.VMEM((rows if rows > BLOCK else 8, static_width), jnp.float32),
            pltpu.SemaphoreType.DMA((4,)),
            pltpu.SemaphoreType.DMA((n_col - 1,)),
            pltpu.SemaphoreType.DMA((n_col - 1,)),
            pltpu.SemaphoreType.DMA((3, n_row // 2, pieces)),
            pltpu.SemaphoreType.DMA((n_row // 2, pieces)),
            pltpu.SemaphoreType.DMA((n_row, pieces)),
        ],
        compiler_params=pltpu.CompilerParams(
            collective_id=0, has_side_effects=True, vmem_limit_bytes=40 * 1024 * 1024),
        cost_estimate=pl.CostEstimate(
            flops=2 * static_width * rows * tv_width, bytes_accessed=4 * static_width * tv_width, transcendentals=0),
    )(*(pltpu.with_memory_space_constraint(value, pltpu.HBM) for value in operands))
    parts = 6
    return pl.pallas_call(
        functools.partial(multiply_out, parts),
        out_shape=jax.ShapeDtypeStruct((static_width, tv_width), jnp.float32),
        in_specs=[vmem, vmem],
        out_specs=pl.BlockSpec(memory_space=pltpu.HBM),
        scratch_shapes=[
            pltpu.VMEM((static_width, tv_width), jnp.float32),
            pltpu.SemaphoreType.DMA((parts,)),
        ],
        compiler_params=pltpu.CompilerParams(vmem_limit_bytes=32 * 1024 * 1024),
    )(weighted, gathered)


def solution(mesh):
    return jax.shard_map(
        functools.partial(body, n_row=mesh.shape["row"], n_col=mesh.shape["col"]),
        mesh=mesh,
        in_specs=(P("col", "row"), P("row", "col"), P(), P()),
        out_specs=P("row", "col"),
        check_vma=False,
    )
```
